128 devices in a mesh: sec: 32 (over y, x, core), mpo: 4 (over z).
Axes of the slice: x: 4, y: 4, z: 4, core: 2. Of those that a mesh axis runs over, the one named last changes fastest.
Arguments:
- wavefunction: bfloat16 [32, 256, 256], P('sec')
- block_dims: int32 [32], P('sec'), may hold values from 64 to 256, as said below
- left_env: bfloat16 [32, 24, 256, 256], P('sec', 'mpo'), may hold values from -0.0625 to 0.0625
- right_env: bfloat16 [32, 24, 256, 256], P('sec', 'mpo'), may hold values from -0.375 to 0.375
- task_left: int32 [32, 128], P('sec', 'mpo'), may hold values from 0 to 31, as said below
- task_term: int32 [32, 128], P('sec', 'mpo'), may hold values from 0 to 5
Outputs:
- first_product: float32 [32, 256, 256], P('sec', 'mpo')
- second_product: float32 [32, 256, 256], P('sec', 'mpo')
The draws below stay inside these ranges and needn't reach their ends.
Inputs may be any that keep to these rules, and one draw needn't show every extreme that they name: `block_dims`: some sector reaches 256. `task_left`: within one row's block of 32 columns at most 2 entries name the same left sector, and in every such block one left sector, the same for all blocks, is named exactly 2 times.
All inputs are finite; a program needn't handle non-finite values.
Results may differ from the reference program's by a relative error of at most 0.005.
Values may be sent and summed in bfloat16 or wider, within the bound.
No kernel may reach another device: no remote copies, remote signals or barrier semaphores. Data moves between devices by JAX's collectives and lax.ppermute only.
A program may use at most 128 MiB of HBM per device.

```python
import math
import jax
import jax.numpy as jnp
from jax import lax

BLOCK = 256
TERMS = 24
TASK_DEV = 32
SECTORS = 32
TERMS_DEV = 6
CAP = 2
N_MPO = 4


def draw_wavefunction(key, part):
    key = jax.random.fold_in(key, 11)
    key_base, key_rows, key_cols = jax.random.split(key, 3)
    shape = (SECTORS, BLOCK, BLOCK)
    row_scale = jnp.exp(jax.random.uniform(key_rows, (SECTORS, BLOCK, 1), jnp.float32, math.log(0.5), math.log(2.0)))
    col_scale = jnp.exp(jax.random.uniform(key_cols, (SECTORS, 1, BLOCK), jnp.float32, math.log(0.5), math.log(2.0)))
    sector_pos = jnp.arange(SECTORS, dtype=jnp.float32) / max(SECTORS - 1, 1)
    ramp = jnp.exp(math.log(3.0) * sector_pos)[:, None, None]
    base = jnp.clip(jax.random.normal(key_base, shape, jnp.float32), -6.0, 6.0)
    return (0.5 * base * row_scale * col_scale * ramp).astype(jnp.bfloat16)


def draw_block_dims(key, part):
    key = jax.random.fold_in(key, 12)
    sector_ids = jnp.arange(SECTORS, dtype=jnp.int32)
    lowest = BLOCK // 4 + (BLOCK - BLOCK // 8 - BLOCK // 4) * sector_ids // max(SECTORS - 1, 1)
    spread = jax.random.randint(key, (SECTORS,), 0, BLOCK // 8 + 1, dtype=jnp.int32)
    dims = jnp.minimum(lowest + spread, BLOCK)
    return jnp.where(sector_ids == SECTORS - 1, BLOCK, dims).astype(jnp.int32)


def draw_task_left(key, part):
    key = jax.random.fold_in(key, 13)
    key_hot, key_popular, key_score = jax.random.split(key, 3)
    slot_count = SECTORS * CAP
    candidates = jnp.arange(slot_count, dtype=jnp.int32)
    targets = candidates // CAP
    hot_sector = jax.random.randint(key_hot, (), 0, SECTORS, dtype=jnp.int32)
    popular = jax.random.randint(key_popular, (SECTORS,), 0, 4, dtype=jnp.int32)
    noise = jax.random.randint(key_score, (SECTORS * N_MPO, slot_count), 0, 4096, dtype=jnp.int32)
    scores = noise + popular[targets][None, :] * 4096 + jnp.where(targets == hot_sector, 65536, 0)[None, :]
    scores = scores * slot_count + candidates[None, :]
    unused, chosen = lax.top_k(scores, TASK_DEV)
    picked = (chosen // CAP).astype(jnp.int32)
    return picked.reshape(SECTORS, N_MPO * TASK_DEV)


def with_ends(drawn, own_key, smallest, top_value):
    index_at = [jax.random.randint(jax.random.fold_in(own_key, axis), (), 0, length) for axis, length in enumerate(drawn.shape)]
    longest = drawn.shape.index(max(drawn.shape))
    next_to = index_at[:longest] + [(index_at[longest] + 1) % drawn.shape[longest]] + index_at[longest + 1:]
    return drawn.at[tuple(index_at)].set(smallest).at[tuple(next_to)].set(top_value)


def levels(stream_key, shape, cuts, low, top_value):
    gain = 1.0
    for position, blocks in cuts:
        steps = jax.random.uniform(jax.random.fold_in(jax.random.fold_in(stream_key, 6), position), (blocks,), jnp.float32, low / len(cuts), top_value / len(cuts))
        gain = gain * jnp.repeat(jnp.exp(steps), shape[position] // blocks).reshape((-1,) + (1,) * (len(shape) - 1 - position))
    return gain


def scatter_about(own_key, shape, scale, reach, cuts=(), kind=jnp.bfloat16):
    result = jax.random.normal(own_key, shape, jnp.float32) * scale
    if len(cuts) > 0:
        result = levels(own_key, shape, cuts, -0.22, 0.18) * result
    return jnp.clip(result, min=-reach, max=reach).astype(kind)


def setup_inputs(seed: int = 0) -> dict:
    key_list = jax.random.split(jax.random.key(seed), 7)
    wavefunction = draw_wavefunction(jax.random.fold_in(key_list[6], 71), 0)
    block_dims = draw_block_dims(jax.random.fold_in(key_list[6], 71), 0)
    left_env = scatter_about(key_list[2], (SECTORS, TERMS, BLOCK, BLOCK), (BLOCK * TASK_DEV) ** -0.5, 0.0625, ((0, 32), (1, 4)))
    right_env = scatter_about(key_list[3], (SECTORS, TERMS, BLOCK, BLOCK), BLOCK ** -0.5, 0.375, ((0, 32), (1, 4)))
    task_left = draw_task_left(jax.random.fold_in(key_list[6], 71), 0)
    task_term = with_ends(jax.random.randint(key_list[5], (SECTORS, N_MPO * TASK_DEV), 0, TERMS_DEV), jax.random.fold_in(key_list[5], 1), 0, TERMS_DEV - 1).astype(jnp.int32)
    return dict(wavefunction=wavefunction, block_dims=block_dims, left_env=left_env, right_env=right_env, task_left=task_left, task_term=task_term)


def live_masks(block_dims):
    positions = jnp.arange(BLOCK, dtype=jnp.int32)
    row_live = positions[None, :, None] < block_dims[:, None, None]
    col_live = positions[None, None, :] < block_dims[:, None, None]
    return row_live & col_live

def apply_hamiltonian(vector, live_mask, left_env, right_env, task_left, term_ids):

    def add_source(total, inputs):
        source_block, source_env, targets, source_terms = inputs
        picked = source_env[source_terms].astype(jnp.float32)
        carried = jnp.einsum('ij,tjk->tik', source_block.astype(jnp.float32), picked).astype(jnp.bfloat16)
        left_blocks = left_env[targets, source_terms].astype(jnp.float32)
        contrib = jnp.einsum('tij,tjk->tik', left_blocks, carried.astype(jnp.float32))
        return (total.at[targets].add(contrib), None)
    start = jnp.zeros((SECTORS, BLOCK, BLOCK), jnp.float32)
    total, unused = lax.scan(add_source, start, (vector, right_env, task_left, term_ids))
    return jnp.where(live_mask, total, jnp.float32(0.0))

def reference(wavefunction, block_dims, left_env, right_env, task_left, task_term):
    live_mask = live_masks(block_dims)
    psi_live = jnp.where(live_mask, wavefunction, jnp.zeros_like(wavefunction)).astype(jnp.bfloat16)
    groups = (jnp.arange(N_MPO * TASK_DEV, dtype=jnp.int32) // TASK_DEV).astype(jnp.int32)
    term_ids = (groups[None, :] * TERMS_DEV + task_term).astype(jnp.int32)
    first_product = apply_hamiltonian(psi_live, live_mask, left_env, right_env, task_left, term_ids)
    square_sum = jnp.sum(first_product * first_product)
    inverse_rms = lax.rsqrt(square_sum / (SECTORS * BLOCK * BLOCK) + 1e-06)
    new_basis = (first_product * inverse_rms).astype(jnp.bfloat16)
    second_product = apply_hamiltonian(new_basis, live_mask, left_env, right_env, task_left, term_ids)
    return (first_product, second_product)
```

```python
import jax
import jax.numpy as jnp
from jax import lax
from jax.experimental import pallas as pl
from jax.experimental.pallas import tpu as pltpu
from jax.sharding import PartitionSpec as P

BLOCK = 256
SECTORS = 32
GROUPS = 4
TERMS = 6
HALF_TERMS = 3
TASKS = 32
SLAB = 16
SLABS = BLOCK // SLAB
SHARE = BLOCK // GROUPS
LANES = 128
DATA_ROWS = HALF_TERMS * 2 * SLAB
SIDE_ROWS = 16
MIX = SECTORS * SLAB
EPSILON = 1e-06
LIFT = 512.0

F32 = jnp.float32
BF16 = jnp.bfloat16
VMEM = pl.BlockSpec(memory_space=pltpu.VMEM)
SMEM = pl.BlockSpec(memory_space=pltpu.SMEM)
PARAMS = pltpu.CompilerParams(vmem_limit_bytes=48 * 1024 * 1024)


def store_carried(vector, right_ref, out_ref):
    for term in range(TERMS):
        half, place = term // HALF_TERMS, term % HALF_TERMS
        carried = jnp.dot(vector, right_ref[0, term], preferred_element_type=F32).astype(BF16)
        for side in range(2):
            row = (place * 2 + side) * SLAB
            part = carried[:, side * LANES : (side + 1) * LANES].reshape(SLABS, SLAB, LANES)
            out_ref[:, half, row : row + SLAB, :] = part


def first_carry_kernel(dims_ref, vector_ref, right_ref, left_ref, term_ref, out_ref):
    live = dims_ref[0]
    rows = lax.broadcasted_iota(jnp.int32, (BLOCK, BLOCK), 0)
    cols = lax.broadcasted_iota(jnp.int32, (BLOCK, BLOCK), 1)
    vector = jnp.where((rows < live) & (cols < live), vector_ref[0].astype(F32), 0.0).astype(BF16)
    store_carried(vector, right_ref, out_ref)
    targets = left_ref[...]
    terms = term_ref[...]
    for half in range(2):
        place = terms - half * HALF_TERMS
        inside = (place >= 0) & (place < HALF_TERMS)
        code = jnp.where(inside, targets + place * SECTORS, 255).astype(F32)
        code = jnp.broadcast_to(code, (SIDE_ROWS, TASKS)).astype(BF16)
        for slab in range(SLABS):
            out_ref[slab, half, DATA_ROWS:, :] = jnp.zeros((SIDE_ROWS, LANES), BF16)
            out_ref[slab, half, DATA_ROWS:, :TASKS] = code


def first_carry(dims, vector, right, left, term):
    return pl.pallas_call(
        first_carry_kernel,
        out_shape=jax.ShapeDtypeStruct((SLABS, 2, DATA_ROWS + SIDE_ROWS, LANES), BF16),
        in_specs=[SMEM, VMEM, VMEM, VMEM, VMEM],
        out_specs=VMEM,
        compiler_params=PARAMS,
        name="first_carry",
    )(dims, vector, right, left, term)


def mix_with(weights_ref, in_ref, out_ref, scale):
    for place in range(HALF_TERMS):
        parts = []
        for side in range(2):
            row = (place * 2 + side) * SLAB
            parts.append(in_ref[:, row : row + SLAB, :].reshape(MIX, LANES))
        mixed = jnp.dot(
            weights_ref[place], jnp.concatenate(parts, axis=1), preferred_element_type=F32
        )
        if scale is not None:
            mixed = jnp.where(scale > 0.0, mixed * scale, 0.0)
        mixed = mixed.astype(BF16).reshape(SECTORS, SLAB, BLOCK)
        out_ref[:, place * SLAB : (place + 1) * SLAB, :] = mixed


def first_mix_kernel(in_ref, out_ref, weights_ref):
    codes = in_ref[:, DATA_ROWS : DATA_ROWS + SIDE_ROWS, :].astype(F32)[:, 0, :]
    lanes = lax.broadcasted_iota(jnp.int32, (SECTORS, LANES), 1).astype(F32)
    counts = jnp.zeros((SECTORS, LANES), F32)
    for task in range(TASKS):
        counts += jnp.where(codes[:, task : task + 1] == lanes, 1.0, 0.0)
    counts = counts.astype(BF16)
    wide_row = lax.broadcasted_iota(jnp.int32, (MIX, LANES), 0) // SLAB
    wide_col = lax.broadcasted_iota(jnp.int32, (MIX, LANES), 1)
    spread = (
        lax.broadcasted_iota(jnp.int32, (SECTORS, MIX), 0)
        == lax.broadcasted_iota(jnp.int32, (SECTORS, MIX), 1) // SLAB
    )
    spread = jnp.where(spread, 1.0, 0.0).astype(BF16)
    same_row = (
        lax.broadcasted_iota(jnp.int32, (MIX, MIX), 0) % SLAB
        == lax.broadcasted_iota(jnp.int32, (MIX, MIX), 1) % SLAB
    )
    for place in range(HALF_TERMS):
        pick = jnp.where(wide_row + place * SECTORS == wide_col, 1.0, 0.0).astype(BF16)
        tall = lax.dot_general(pick, counts, (((1,), (1,)), ((), ())), preferred_element_type=F32)
        full = jnp.dot(tall.astype(BF16), spread, preferred_element_type=F32)
        weights_ref[place] = jnp.where(same_row, full, 0.0).astype(BF16)
    mix_with(weights_ref, in_ref, out_ref, None)


def first_mix(received):
    return pl.pallas_call(
        first_mix_kernel,
        out_shape=(
            jax.ShapeDtypeStruct((SECTORS, HALF_TERMS * SLAB, BLOCK), BF16),
            jax.ShapeDtypeStruct((HALF_TERMS, MIX, MIX), BF16),
        ),
        in_specs=[VMEM],
        out_specs=(VMEM, VMEM),
        compiler_params=PARAMS,
        name="first_mix",
    )(received)


def second_mix_kernel(in_ref, weights_ref, out_ref):
    pieces = in_ref[:, DATA_ROWS : DATA_ROWS + SIDE_ROWS, :].astype(F32)
    mean = jnp.sum(pieces, keepdims=True)[0]
    inverse_rms = lax.rsqrt(mean + EPSILON) * (1.0 / LIFT)
    mix_with(weights_ref, in_ref, out_ref, inverse_rms)


def second_mix(received, weights):
    return pl.pallas_call(
        second_mix_kernel,
        out_shape=jax.ShapeDtypeStruct((SECTORS, HALF_TERMS * SLAB, BLOCK), BF16),
        in_specs=[VMEM, VMEM],
        out_specs=VMEM,
        compiler_params=PARAMS,
        name="second_mix",
    )(received, weights)


def left_kernel(group_ref, in_ref, left_ref, *refs):
    *out_refs, total = refs
    value = jnp.zeros((BLOCK, BLOCK), F32)
    for term in range(TERMS):
        half, place = term // HALF_TERMS, term % HALF_TERMS
        mixed = in_ref[:, half, place * SLAB : (place + 1) * SLAB, :].reshape(BLOCK, BLOCK)
        value += jnp.dot(left_ref[0, term], mixed, preferred_element_type=F32)
    total[...] = value
    for step in range(GROUPS):
        owner = lax.rem(group_ref[0] + step, GROUPS)
        out_refs[step][...] = total[pl.ds(pl.multiple_of(owner * SHARE, SHARE), SHARE), :]


def apply_left(group, received, left_env):
    share = jax.ShapeDtypeStruct((SHARE, BLOCK), F32)
    return pl.pallas_call(
        left_kernel,
        out_shape=(share,) * GROUPS,
        in_specs=[SMEM, VMEM, VMEM],
        out_specs=(VMEM,) * GROUPS,
        scratch_shapes=[pltpu.VMEM((BLOCK, BLOCK), F32)],
        compiler_params=PARAMS,
        name="apply_left",
    )(group, received.reshape(SLABS, 2, HALF_TERMS * SLAB, BLOCK), left_env)


def live_sum(group_ref, dims_ref, part_refs):
    live = dims_ref[0]
    rows = lax.broadcasted_iota(jnp.int32, (SHARE, BLOCK), 0) + group_ref[0] * SHARE
    cols = lax.broadcasted_iota(jnp.int32, (SHARE, BLOCK), 1)
    value = (part_refs[0][...] + part_refs[1][...]) + (part_refs[2][...] + part_refs[3][...])
    return jnp.where((rows < live) & (cols < live), value, 0.0)


def first_sum_kernel(group_ref, dims_ref, *refs):
    *part_refs, out_ref, basis_ref = refs
    value = live_sum(group_ref, dims_ref, part_refs)
    out_ref[0] = value
    basis_ref[:SHARE, :] = (value * LIFT).astype(BF16)
    mean = jnp.sum(value * value, keepdims=True) * (1.0 / (SECTORS * BLOCK * BLOCK))
    high = mean.astype(BF16)
    rest = jnp.where(mean < jnp.inf, mean - high.astype(F32), 0.0)
    middle = rest.astype(BF16)
    low = (rest - middle.astype(F32)).astype(BF16)
    lane = lax.broadcasted_iota(jnp.int32, (SIDE_ROWS, BLOCK), 1)
    row = lax.broadcasted_iota(jnp.int32, (SIDE_ROWS, BLOCK), 0)
    pieces = jnp.where(lane == 0, high.astype(F32), 0.0)
    pieces = jnp.where(lane == 1, middle.astype(F32), pieces)
    pieces = jnp.where(lane == 2, low.astype(F32), pieces)
    basis_ref[SHARE:, :] = jnp.where(row == 0, pieces, 0.0).astype(BF16)


def first_sum(group, dims, parts):
    return pl.pallas_call(
        first_sum_kernel,
        out_shape=(
            jax.ShapeDtypeStruct((1, SHARE, BLOCK), F32),
            jax.ShapeDtypeStruct((SHARE + SIDE_ROWS, BLOCK), BF16),
        ),
        in_specs=[SMEM, SMEM] + [VMEM] * GROUPS,
        out_specs=(VMEM, VMEM),
        compiler_params=PARAMS,
        name="first_sum",
    )(group, dims, *parts)


def second_sum_kernel(group_ref, dims_ref, *refs):
    *part_refs, out_ref = refs
    out_ref[0] = live_sum(group_ref, dims_ref, part_refs)


def second_sum(group, dims, parts):
    return pl.pallas_call(
        second_sum_kernel,
        out_shape=jax.ShapeDtypeStruct((1, SHARE, BLOCK), F32),
        in_specs=[SMEM, SMEM] + [VMEM] * GROUPS,
        out_specs=VMEM,
        compiler_params=PARAMS,
        name="second_sum",
    )(group, dims, *parts)


def second_carry_kernel(group_ref, right_ref, *refs):
    *part_refs, out_ref, vector_ref = refs
    pieces = jnp.zeros((SIDE_ROWS, LANES), F32)
    lane = lax.broadcasted_iota(jnp.int32, (SIDE_ROWS, LANES), 1)
    for step in range(GROUPS):
        owner = lax.rem(group_ref[0] + GROUPS - step, GROUPS)
        rows = pl.ds(pl.multiple_of(owner * SHARE, SHARE), SHARE)
        vector_ref[rows, :] = part_refs[step][:SHARE, :]
        got = part_refs[step][SHARE:, :LANES].astype(F32)
        pieces += got if step == 0 else pltpu.roll(got, 3 * step, 1)
    store_carried(vector_ref[...], right_ref, out_ref)
    pieces = jnp.where(lane < 3 * GROUPS, pieces, 0.0).astype(BF16)
    for slab in range(SLABS):
        for half in range(2):
            out_ref[slab, half, DATA_ROWS:, :] = pieces


def second_carry(group, right, parts):
    return pl.pallas_call(
        second_carry_kernel,
        out_shape=jax.ShapeDtypeStruct((SLABS, 2, DATA_ROWS + SIDE_ROWS, LANES), BF16),
        in_specs=[SMEM, VMEM] + [VMEM] * GROUPS,
        out_specs=VMEM,
        scratch_shapes=[pltpu.VMEM((BLOCK, BLOCK), BF16)],
        compiler_params=PARAMS,
        name="second_carry",
    )(group, right, *parts)


def exchange(messages):
    messages = messages.reshape((SECTORS,) + messages.shape[-2:])
    return lax.all_to_all(messages, "sec", split_axis=0, concat_axis=0, tiled=True)


def shift(value, step):
    pairs = [(group, (group + step) % GROUPS) for group in range(GROUPS)]
    return lax.ppermute(value, "mpo", pairs)


def body(wavefunction, block_dims, left_env, right_env, task_left, task_term):
    group = lax.axis_index("mpo").astype(jnp.int32).reshape(1)
    carried = first_carry(block_dims, wavefunction, right_env, task_left, task_term)
    mixed, weights = first_mix(exchange(carried))
    parts = apply_left(group, exchange(mixed), left_env)
    parts = [parts[0]] + [shift(parts[step], step) for step in range(1, GROUPS)]
    first_product, basis = first_sum(group, block_dims, parts)
    parts = [basis] + [shift(basis, step) for step in range(1, GROUPS)]
    carried = second_carry(group, right_env, parts)
    mixed = second_mix(exchange(carried), weights)
    parts = apply_left(group, exchange(mixed), left_env)
    parts = [parts[0]] + [shift(parts[step], step) for step in range(1, GROUPS)]
    second_product = second_sum(group, block_dims, parts)
    return (first_product, second_product)


def solution(mesh):
    in_specs = (
        P("sec", None, None),
        P("sec"),
        P("sec", "mpo", None, None),
        P("sec", "mpo", None, None),
        P("sec", "mpo"),
        P("sec", "mpo"),
    )
    out_specs = (P("sec", "mpo", None), P("sec", "mpo", None))
    return jax.shard_map(body, mesh=mesh, in_specs=in_specs, out_specs=out_specs, check_vma=False)
```

```python
import jax
import jax.numpy as jnp
from jax import lax
from jax.experimental import pallas as pl
from jax.experimental.pallas import tpu as pltpu
from jax.sharding import PartitionSpec as P

BLOCK = 256
SECTORS = 32
GROUPS = 4
TERMS = 6
HALF_TERMS = 3
TASKS = 32
SLAB = 16
SLABS = BLOCK // SLAB
SHARE = BLOCK // GROUPS
LANES = 128
DATA_ROWS = HALF_TERMS * 2 * SLAB
SIDE_ROWS = 16
MIX = SECTORS * SLAB
EPSILON = 1e-06
LIFT = 512.0

F32 = jnp.float32
BF16 = jnp.bfloat16
VMEM = pl.BlockSpec(memory_space=pltpu.VMEM)
SMEM = pl.BlockSpec(memory_space=pltpu.SMEM)
HBM = pl.BlockSpec(memory_space=pltpu.HBM)
PARAMS = pltpu.CompilerParams(vmem_limit_bytes=48 * 1024 * 1024)


def store_carried(term, carried, out_ref):
    half, place = term // HALF_TERMS, term % HALF_TERMS
    carried = carried.astype(BF16)
    for side in range(2):
        row = (place * 2 + side) * SLAB
        part = carried[:, side * LANES : (side + 1) * LANES].reshape(SLABS, SLAB, LANES)
        out_ref[:, half, row : row + SLAB, :] = part


def first_carry_kernel(
    dims_ref, group_ref, vector_hbm, right_hbm, left_hbm, term_hbm, out_ref, vector_ref, right_ref, left_ref, term_ref, sems
):
    del group_ref
    copies = [
        pltpu.make_async_copy(left_hbm, left_ref, sems.at[TERMS]),
        pltpu.make_async_copy(term_hbm, term_ref, sems.at[TERMS + 1]),
        pltpu.make_async_copy(vector_hbm, vector_ref, sems.at[TERMS + 2]),
    ]
    fetches = [
        pltpu.make_async_copy(right_hbm.at[0, term], right_ref.at[0, term], sems.at[term])
        for term in range(TERMS)
    ]
    for copy in copies + fetches:
        copy.start()
    copies[0].wait()
    copies[1].wait()
    targets = left_ref[...]
    terms = term_ref[...]
    for half in range(2):
        place = terms - half * HALF_TERMS
        inside = (place >= 0) & (place < HALF_TERMS)
        code = jnp.where(inside, targets + place * SECTORS, 255).astype(F32)
        code = jnp.broadcast_to(code, (SIDE_ROWS, TASKS)).astype(BF16)
        for slab in range(SLABS):
            out_ref[slab, half, DATA_ROWS:, :] = jnp.zeros((SIDE_ROWS, LANES), BF16)
            out_ref[slab, half, DATA_ROWS:, :TASKS] = code
    copies[2].wait()
    live = dims_ref[0]
    rows = lax.broadcasted_iota(jnp.int32, (BLOCK, BLOCK), 0)
    cols = lax.broadcasted_iota(jnp.int32, (BLOCK, BLOCK), 1)
    vector = jnp.where((rows < live) & (cols < live), vector_ref[0].astype(F32), 0.0).astype(BF16)
    for term in range(TERMS):
        fetches[term].wait()
        carried = jnp.dot(vector, right_ref[0, term], preferred_element_type=F32)
        store_carried(term, carried, out_ref)


def first_carry(dims, group, vector, right, left, term):
    return pl.pallas_call(
        first_carry_kernel,
        out_shape=jax.ShapeDtypeStruct((SLABS, 2, DATA_ROWS + SIDE_ROWS, LANES), BF16),
        in_specs=[SMEM, SMEM, HBM, HBM, HBM, HBM],
        out_specs=VMEM,
        scratch_shapes=[
            pltpu.VMEM((1, BLOCK, BLOCK), BF16),
            pltpu.VMEM((1, TERMS, BLOCK, BLOCK), BF16),
            pltpu.VMEM((1, TASKS), jnp.int32),
            pltpu.VMEM((1, TASKS), jnp.int32),
            pltpu.SemaphoreType.DMA((TERMS + 3,)),
        ],
        compiler_params=PARAMS,
        name="first_carry",
    )(dims, group, vector, right, left, term)


def mix_with(weights_ref, in_ref, out_ref, scale):
    for place in range(HALF_TERMS):
        parts = []
        for side in range(2):
            row = (place * 2 + side) * SLAB
            parts.append(in_ref[:, row : row + SLAB, :].reshape(MIX, LANES))
        mixed = jnp.dot(
            weights_ref[place], jnp.concatenate(parts, axis=1), preferred_element_type=F32
        )
        if scale is not None:
            mixed = jnp.where(scale > 0.0, mixed * scale, 0.0)
        mixed = mixed.astype(BF16).reshape(SECTORS, SLAB, BLOCK)
        out_ref[:, place * SLAB : (place + 1) * SLAB, :] = mixed


def first_mix_kernel(in_ref, out_ref, weights_ref, wide_ref):
    codes = in_ref[:, DATA_ROWS : DATA_ROWS + SIDE_ROWS, :].astype(F32)[:, 0, :]
    lanes = lax.broadcasted_iota(jnp.int32, (SECTORS, LANES), 1).astype(F32)
    counts = jnp.zeros((SECTORS, LANES), F32)
    for task in range(TASKS):
        counts += jnp.where(codes[:, task : task + 1] == lanes, 1.0, 0.0)
    counts = counts.astype(BF16)
    spread = (
        lax.broadcasted_iota(jnp.int32, (SECTORS, MIX), 0)
        == lax.broadcasted_iota(jnp.int32, (SECTORS, MIX), 1) // SLAB
    )
    spread = jnp.where(spread, 1.0, 0.0).astype(BF16)
    wide_ref[...] = lax.dot_general(
        counts, spread, (((0,), (0,)), ((), ())), preferred_element_type=F32
    )
    same_row = (
        lax.broadcasted_iota(jnp.int32, (SLAB, MIX), 0)
        == lax.broadcasted_iota(jnp.int32, (SLAB, MIX), 1) % SLAB
    )
    same_row = jnp.where(same_row, 1.0, 0.0)
    for place in range(HALF_TERMS):
        for target in range(SECTORS):
            line = place * SECTORS + target
            weights_ref[place, target * SLAB : (target + 1) * SLAB, :] = (
                same_row * wide_ref[line : line + 1, :]
            ).astype(BF16)
    mix_with(weights_ref, in_ref, out_ref, None)


def first_mix(received):
    return pl.pallas_call(
        first_mix_kernel,
        out_shape=(
            jax.ShapeDtypeStruct((SECTORS, HALF_TERMS * SLAB, BLOCK), BF16),
            jax.ShapeDtypeStruct((HALF_TERMS, MIX, MIX), BF16),
        ),
        in_specs=[VMEM],
        out_specs=(VMEM, VMEM),
        scratch_shapes=[pltpu.VMEM((LANES, MIX), F32)],
        compiler_params=PARAMS,
        name="first_mix",
    )(received)


def second_mix_kernel(in_ref, weights_ref, out_ref):
    pieces = in_ref[:, DATA_ROWS : DATA_ROWS + SIDE_ROWS, :].astype(F32)
    mean = jnp.sum(pieces, keepdims=True)[0]
    inverse_rms = lax.rsqrt(mean + EPSILON) * (1.0 / LIFT)
    mix_with(weights_ref, in_ref, out_ref, inverse_rms)


def second_mix(received, weights):
    return pl.pallas_call(
        second_mix_kernel,
        out_shape=jax.ShapeDtypeStruct((SECTORS, HALF_TERMS * SLAB, BLOCK), BF16),
        in_specs=[VMEM, VMEM],
        out_specs=VMEM,
        compiler_params=PARAMS,
        name="second_mix",
    )(received, weights)


def left_product(in_ref, left_ref):
    value = jnp.zeros((BLOCK, BLOCK), F32)
    for term in range(TERMS):
        half, place = term // HALF_TERMS, term % HALF_TERMS
        mixed = in_ref[:, half, place * SLAB : (place + 1) * SLAB, :].reshape(BLOCK, BLOCK)
        value += jnp.dot(left_ref[0, term], mixed, preferred_element_type=F32)
    return value


def first_left_kernel(in_ref, left_ref, own_ref, sent_ref):
    value = left_product(in_ref, left_ref)
    own_ref[...] = value
    sent_ref[...] = value.astype(BF16)


def first_left(received, left_env):
    return pl.pallas_call(
        first_left_kernel,
        out_shape=(
            jax.ShapeDtypeStruct((BLOCK, BLOCK), F32),
            jax.ShapeDtypeStruct((BLOCK, BLOCK), BF16),
        ),
        in_specs=[VMEM, VMEM],
        out_specs=(VMEM, VMEM),
        compiler_params=PARAMS,
        name="first_left",
    )(received.reshape(SLABS, 2, HALF_TERMS * SLAB, BLOCK), left_env)


def second_left_kernel(group_ref, in_ref, left_ref, *refs):
    *out_refs, total = refs
    total[...] = left_product(in_ref, left_ref)
    for step in range(GROUPS):
        owner = lax.rem(group_ref[0] + step, GROUPS)
        out_refs[step][...] = total[pl.ds(pl.multiple_of(owner * SHARE, SHARE), SHARE), :]


def second_left(group, received, left_env):
    share = jax.ShapeDtypeStruct((SHARE, BLOCK), F32)
    return pl.pallas_call(
        second_left_kernel,
        out_shape=(share,) * GROUPS,
        in_specs=[SMEM, VMEM, VMEM],
        out_specs=(VMEM,) * GROUPS,
        scratch_shapes=[pltpu.VMEM((BLOCK, BLOCK), F32)],
        compiler_params=PARAMS,
        name="second_left",
    )(group, received.reshape(SLABS, 2, HALF_TERMS * SLAB, BLOCK), left_env)


def live_only(value, first_row, live):
    rows = lax.broadcasted_iota(jnp.int32, value.shape, 0) + first_row
    cols = lax.broadcasted_iota(jnp.int32, value.shape, 1)
    return jnp.where((rows < live) & (cols < live), value, 0.0)


def second_carry_kernel(group_ref, dims_ref, right_ref, own_ref, *refs):
    *part_refs, out_ref, first_hbm, total, sem = refs
    value = own_ref[...]
    for part_ref in part_refs:
        value += part_ref[...].astype(F32)
    value = live_only(value, 0, dims_ref[0])
    total[...] = value
    first_row = pl.multiple_of(group_ref[0] * SHARE, SHARE)
    copy = pltpu.make_async_copy(total.at[pl.ds(first_row, SHARE), :], first_hbm.at[0], sem)
    copy.start()
    mean = jnp.sum(value * value, keepdims=True) * (1.0 / (SECTORS * BLOCK * BLOCK))
    high = mean.astype(BF16)
    rest = jnp.where(mean < jnp.inf, mean - high.astype(F32), 0.0)
    middle = rest.astype(BF16)
    low = (rest - middle.astype(F32)).astype(BF16)
    lane = lax.broadcasted_iota(jnp.int32, (SIDE_ROWS, LANES), 1)
    row = lax.broadcasted_iota(jnp.int32, (SIDE_ROWS, LANES), 0)
    pieces = jnp.where(lane == 0, high.astype(F32), 0.0)
    pieces = jnp.where(lane == 1, middle.astype(F32), pieces)
    pieces = jnp.where(lane == 2, low.astype(F32), pieces)
    pieces = jnp.where(row == 0, pieces, 0.0).astype(BF16)
    for slab in range(SLABS):
        for half in range(2):
            out_ref[slab, half, DATA_ROWS:, :] = pieces
    lifted = value * LIFT
    upper = lifted.astype(BF16)
    lower = (lifted - upper.astype(F32)).astype(BF16)
    for term in range(TERMS):
        right = right_ref[0, term]
        carried = jnp.dot(upper, right, preferred_element_type=F32)
        carried += jnp.dot(lower, right, preferred_element_type=F32)
        store_carried(term, carried, out_ref)
    copy.wait()


def second_carry(group, dims, right, own, parts):
    return pl.pallas_call(
        second_carry_kernel,
        out_shape=(
            jax.ShapeDtypeStruct((SLABS, 2, DATA_ROWS + SIDE_ROWS, LANES), BF16),
            jax.ShapeDtypeStruct((1, SHARE, BLOCK), F32),
        ),
        in_specs=[SMEM, SMEM] + [VMEM] * (GROUPS + 1),
        out_specs=(VMEM, HBM),
        scratch_shapes=[pltpu.VMEM((BLOCK, BLOCK), F32), pltpu.SemaphoreType.DMA],
        compiler_params=PARAMS,
        name="second_carry",
    )(group, dims, right, own, *parts)


def second_sum_kernel(group_ref, dims_ref, *refs):
    *part_refs, out_ref = refs
    value = (part_refs[0][...] + part_refs[1][...]) + (part_refs[2][...] + part_refs[3][...])
    out_ref[0] = live_only(value, group_ref[0] * SHARE, dims_ref[0])


def second_sum(group, dims, parts):
    return pl.pallas_call(
        second_sum_kernel,
        out_shape=jax.ShapeDtypeStruct((1, SHARE, BLOCK), F32),
        in_specs=[SMEM, SMEM] + [VMEM] * GROUPS,
        out_specs=VMEM,
        compiler_params=PARAMS,
        name="second_sum",
    )(group, dims, *parts)


def exchange(messages):
    messages = messages.reshape((SECTORS,) + messages.shape[-2:])
    return lax.all_to_all(messages, "sec", split_axis=0, concat_axis=0, tiled=True)


def shift(value, step):
    pairs = [(group, (group + step) % GROUPS) for group in range(GROUPS)]
    return lax.ppermute(value, "mpo", pairs)


def body(wavefunction, block_dims, left_env, right_env, task_left, task_term):
    group = lax.axis_index("mpo").astype(jnp.int32).reshape(1)
    carried = first_carry(block_dims, group, wavefunction, right_env, task_left, task_term)
    mixed, weights = first_mix(exchange(carried))
    own, sent = first_left(exchange(mixed), left_env)
    parts = [shift(sent, step) for step in range(1, GROUPS)]
    carried, first_product = second_carry(group, block_dims, right_env, own, parts)
    mixed = second_mix(exchange(carried), weights)
    parts = second_left(group, exchange(mixed), left_env)
    parts = [parts[0]] + [shift(parts[step], step) for step in range(1, GROUPS)]
    second_product = second_sum(group, block_dims, parts)
    return (first_product, second_product)


def solution(mesh):
    in_specs = (
        P("sec", None, None),
        P("sec"),
        P("sec", "mpo", None, None),
        P("sec", "mpo", None, None),
        P("sec", "mpo"),
        P("sec", "mpo"),
    )
    out_specs = (P("sec", "mpo", None), P("sec", "mpo", None))
    return jax.shard_map(body, mesh=mesh, in_specs=in_specs, out_specs=out_specs, check_vma=False)
```

```python
import jax
import jax.numpy as jnp
from jax import lax
from jax.experimental import pallas as pl
from jax.experimental.pallas import tpu as pltpu
from jax.sharding import PartitionSpec as P

BLOCK = 256
SECTORS = 32
GROUPS = 4
TERMS = 6
HALF_TERMS = 3
TASKS = 32
SLAB = 16
SLABS = BLOCK // SLAB
SHARE = BLOCK // GROUPS
LANES = 128
DATA_ROWS = HALF_TERMS * 2 * SLAB
SIDE_ROWS = 8
MIX = SECTORS * SLAB
EPSILON = 1e-06
LIFT = 512.0

F32 = jnp.float32
BF16 = jnp.bfloat16
VMEM = pl.BlockSpec(memory_space=pltpu.VMEM)
SMEM = pl.BlockSpec(memory_space=pltpu.SMEM)
HBM = pl.BlockSpec(memory_space=pltpu.HBM)
PARAMS = pltpu.CompilerParams(vmem_limit_bytes=48 * 1024 * 1024)


def store_carried(term, carried, out_ref):
    half, place = term // HALF_TERMS, term % HALF_TERMS
    carried = carried.astype(BF16)
    for side in range(2):
        row = (place * 2 + side) * SLAB
        part = carried[:, side * LANES : (side + 1) * LANES].reshape(SLABS, SLAB, LANES)
        out_ref[:, half, row : row + SLAB, :] = part


def first_carry_kernel(
    dims_ref, group_ref, vector_hbm, right_hbm, left_hbm, term_hbm, out_ref, vector_ref, right_ref, left_ref, term_ref, sems
):
    del group_ref
    copies = [
        pltpu.make_async_copy(left_hbm, left_ref, sems.at[TERMS]),
        pltpu.make_async_copy(term_hbm, term_ref, sems.at[TERMS + 1]),
        pltpu.make_async_copy(vector_hbm, vector_ref, sems.at[TERMS + 2]),
    ]
    fetches = [
        pltpu.make_async_copy(right_hbm.at[0, term], right_ref.at[0, term], sems.at[term])
        for term in range(TERMS)
    ]
    for copy in copies + fetches:
        copy.start()
    copies[0].wait()
    copies[1].wait()
    targets = left_ref[...]
    terms = term_ref[...]
    for half in range(2):
        place = terms - half * HALF_TERMS
        inside = (place >= 0) & (place < HALF_TERMS)
        code = jnp.where(inside, targets + place * SECTORS, 255).astype(F32)
        code = jnp.broadcast_to(code, (SIDE_ROWS, TASKS)).astype(BF16)
        for slab in range(SLABS):
            out_ref[slab, half, DATA_ROWS:, :] = jnp.zeros((SIDE_ROWS, LANES), BF16)
            out_ref[slab, half, DATA_ROWS:, :TASKS] = code
    copies[2].wait()
    live = dims_ref[0]
    rows = lax.broadcasted_iota(jnp.int32, (BLOCK, BLOCK), 0)
    cols = lax.broadcasted_iota(jnp.int32, (BLOCK, BLOCK), 1)
    vector = jnp.where((rows < live) & (cols < live), vector_ref[0].astype(F32), 0.0).astype(BF16)
    for term in range(TERMS):
        fetches[term].wait()
        carried = jnp.dot(vector, right_ref[0, term], preferred_element_type=F32)
        store_carried(term, carried, out_ref)


def first_carry(dims, group, *fetched):
    fetched = [pltpu.with_memory_space_constraint(array, pltpu.HBM) for array in fetched]
    return pl.pallas_call(
        first_carry_kernel,
        out_shape=jax.ShapeDtypeStruct((SLABS, 2, DATA_ROWS + SIDE_ROWS, LANES), BF16),
        in_specs=[SMEM, SMEM, HBM, HBM, HBM, HBM],
        out_specs=VMEM,
        scratch_shapes=[
            pltpu.VMEM((1, BLOCK, BLOCK), BF16),
            pltpu.VMEM((1, TERMS, BLOCK, BLOCK), BF16),
            pltpu.VMEM((1, TASKS), jnp.int32),
            pltpu.VMEM((1, TASKS), jnp.int32),
            pltpu.SemaphoreType.DMA((TERMS + 3,)),
        ],
        compiler_params=PARAMS,
        name="first_carry",
    )(dims, group, *fetched)


def mix_with(weights_ref, in_ref, out_ref, scale):
    for place in range(HALF_TERMS):
        parts = []
        for side in range(2):
            row = (place * 2 + side) * SLAB
            parts.append(in_ref[:, row : row + SLAB, :].reshape(MIX, LANES))
        mixed = jnp.dot(
            weights_ref[place], jnp.concatenate(parts, axis=1), preferred_element_type=F32
        )
        if scale is not None:
            mixed = jnp.where(scale > 0.0, mixed * scale, 0.0)
        mixed = mixed.astype(BF16).reshape(SECTORS, SLAB, BLOCK)
        out_ref[:, place * SLAB : (place + 1) * SLAB, :] = mixed


def first_mix_kernel(in_ref, out_ref, weights_ref, wide_ref):
    codes = in_ref[:, DATA_ROWS : DATA_ROWS + SIDE_ROWS, :].astype(F32)[:, 0, :]
    lanes = lax.broadcasted_iota(jnp.int32, (SECTORS, LANES), 1).astype(F32)
    counts = jnp.zeros((SECTORS, LANES), F32)
    for task in range(TASKS):
        counts += jnp.where(codes[:, task : task + 1] == lanes, 1.0, 0.0)
    counts = counts.astype(BF16)
    spread = (
        lax.broadcasted_iota(jnp.int32, (SECTORS, MIX), 0)
        == lax.broadcasted_iota(jnp.int32, (SECTORS, MIX), 1) // SLAB
    )
    spread = jnp.where(spread, 1.0, 0.0).astype(BF16)
    wide_ref[...] = lax.dot_general(
        counts, spread, (((0,), (0,)), ((), ())), preferred_element_type=F32
    )
    same_row = (
        lax.broadcasted_iota(jnp.int32, (SLAB, MIX), 0)
        == lax.broadcasted_iota(jnp.int32, (SLAB, MIX), 1) % SLAB
    )
    same_row = jnp.where(same_row, 1.0, 0.0)
    for place in range(HALF_TERMS):
        for target in range(SECTORS):
            line = place * SECTORS + target
            weights_ref[place, target * SLAB : (target + 1) * SLAB, :] = (
                same_row * wide_ref[line : line + 1, :]
            ).astype(BF16)
    mix_with(weights_ref, in_ref, out_ref, None)


def first_mix(received):
    return pl.pallas_call(
        first_mix_kernel,
        out_shape=(
            jax.ShapeDtypeStruct((SECTORS, HALF_TERMS * SLAB, BLOCK), BF16),
            jax.ShapeDtypeStruct((HALF_TERMS, MIX, MIX), BF16),
        ),
        in_specs=[VMEM],
        out_specs=(VMEM, VMEM),
        scratch_shapes=[pltpu.VMEM((LANES, MIX), F32)],
        compiler_params=PARAMS,
        name="first_mix",
    )(received)


def second_mix_kernel(in_ref, weights_ref, out_ref):
    pieces = in_ref[:, DATA_ROWS : DATA_ROWS + SIDE_ROWS, :].astype(F32)
    mean = jnp.sum(pieces, keepdims=True)[0]
    inverse_rms = lax.rsqrt(mean + EPSILON) * (1.0 / LIFT)
    mix_with(weights_ref, in_ref, out_ref, inverse_rms)


def second_mix(received, weights):
    return pl.pallas_call(
        second_mix_kernel,
        out_shape=jax.ShapeDtypeStruct((SECTORS, HALF_TERMS * SLAB, BLOCK), BF16),
        in_specs=[VMEM, VMEM],
        out_specs=VMEM,
        compiler_params=PARAMS,
        name="second_mix",
    )(received, weights)


def left_product(in_ref, left_ref):
    value = jnp.zeros((BLOCK, BLOCK), F32)
    for term in range(TERMS):
        half, place = term // HALF_TERMS, term % HALF_TERMS
        mixed = in_ref[:, half, place * SLAB : (place + 1) * SLAB, :].reshape(BLOCK, BLOCK)
        value += jnp.dot(left_ref[0, term], mixed, preferred_element_type=F32)
    return value


def first_left_kernel(in_ref, left_ref, own_ref, sent_ref):
    value = left_product(in_ref, left_ref)
    own_ref[...] = value
    sent_ref[...] = value.astype(BF16)


def first_left(received, left_env):
    return pl.pallas_call(
        first_left_kernel,
        out_shape=(
            jax.ShapeDtypeStruct((BLOCK, BLOCK), F32),
            jax.ShapeDtypeStruct((BLOCK, BLOCK), BF16),
        ),
        in_specs=[VMEM, VMEM],
        out_specs=(VMEM, VMEM),
        compiler_params=PARAMS,
        name="first_left",
    )(received.reshape(SLABS, 2, HALF_TERMS * SLAB, BLOCK), left_env)


def second_left_kernel(group_ref, in_ref, left_ref, *refs):
    *out_refs, total = refs
    total[...] = left_product(in_ref, left_ref)
    for step in range(GROUPS):
        owner = lax.rem(group_ref[0] + step, GROUPS)
        part = total[pl.ds(pl.multiple_of(owner * SHARE, SHARE), SHARE), :]
        out_refs[step][...] = part.astype(out_refs[step].dtype)


def second_left(group, received, left_env):
    own = jax.ShapeDtypeStruct((SHARE, BLOCK), F32)
    sent = jax.ShapeDtypeStruct((SHARE, BLOCK), BF16)
    return pl.pallas_call(
        second_left_kernel,
        out_shape=(own,) + (sent,) * (GROUPS - 1),
        in_specs=[SMEM, VMEM, VMEM],
        out_specs=(VMEM,) * GROUPS,
        scratch_shapes=[pltpu.VMEM((BLOCK, BLOCK), F32)],
        compiler_params=PARAMS,
        name="second_left",
    )(group, received.reshape(SLABS, 2, HALF_TERMS * SLAB, BLOCK), left_env)


def live_only(value, first_row, live):
    rows = lax.broadcasted_iota(jnp.int32, value.shape, 0) + first_row
    cols = lax.broadcasted_iota(jnp.int32, value.shape, 1)
    return jnp.where((rows < live) & (cols < live), value, 0.0)


def second_carry_kernel(group_ref, dims_ref, right_ref, own_ref, *refs):
    *part_refs, out_ref, first_hbm, total, sem = refs
    value = own_ref[...]
    for part_ref in part_refs:
        value += part_ref[...].astype(F32)
    value = live_only(value, 0, dims_ref[0])
    total[...] = value
    first_row = pl.multiple_of(group_ref[0] * SHARE, SHARE)
    copy = pltpu.make_async_copy(total.at[pl.ds(first_row, SHARE), :], first_hbm.at[0], sem)
    copy.start()
    mean = jnp.sum(value * value, keepdims=True) * (1.0 / (SECTORS * BLOCK * BLOCK))
    high = mean.astype(BF16)
    rest = jnp.where(mean < jnp.inf, mean - high.astype(F32), 0.0)
    middle = rest.astype(BF16)
    low = (rest - middle.astype(F32)).astype(BF16)
    lane = lax.broadcasted_iota(jnp.int32, (SIDE_ROWS, LANES), 1)
    row = lax.broadcasted_iota(jnp.int32, (SIDE_ROWS, LANES), 0)
    pieces = jnp.where(lane == 0, high.astype(F32), 0.0)
    pieces = jnp.where(lane == 1, middle.astype(F32), pieces)
    pieces = jnp.where(lane == 2, low.astype(F32), pieces)
    pieces = jnp.where(row == 0, pieces, 0.0).astype(BF16)
    for slab in range(SLABS):
        for half in range(2):
            out_ref[slab, half, DATA_ROWS:, :] = pieces
    lifted = value * LIFT
    upper = lifted.astype(BF16)
    lower = (lifted - upper.astype(F32)).astype(BF16)
    for term in range(TERMS):
        right = right_ref[0, term]
        carried = jnp.dot(upper, right, preferred_element_type=F32)
        carried += jnp.dot(lower, right, preferred_element_type=F32)
        store_carried(term, carried, out_ref)
    copy.wait()


def second_carry(group, dims, right, own, parts):
    return pl.pallas_call(
        second_carry_kernel,
        out_shape=(
            jax.ShapeDtypeStruct((SLABS, 2, DATA_ROWS + SIDE_ROWS, LANES), BF16),
            jax.ShapeDtypeStruct((1, SHARE, BLOCK), F32),
        ),
        in_specs=[SMEM, SMEM] + [VMEM] * (GROUPS + 1),
        out_specs=(VMEM, HBM),
        scratch_shapes=[pltpu.VMEM((BLOCK, BLOCK), F32), pltpu.SemaphoreType.DMA],
        compiler_params=PARAMS,
        name="second_carry",
    )(group, dims, right, own, *parts)


def second_sum_kernel(group_ref, dims_ref, *refs):
    *part_refs, out_ref = refs
    value = part_refs[0][...]
    for part_ref in part_refs[1:]:
        value += part_ref[...].astype(F32)
    out_ref[0] = live_only(value, group_ref[0] * SHARE, dims_ref[0])


def second_sum(group, dims, parts):
    return pl.pallas_call(
        second_sum_kernel,
        out_shape=jax.ShapeDtypeStruct((1, SHARE, BLOCK), F32),
        in_specs=[SMEM, SMEM] + [VMEM] * GROUPS,
        out_specs=VMEM,
        compiler_params=PARAMS,
        name="second_sum",
    )(group, dims, *parts)


def exchange(messages):
    messages = messages.reshape((SECTORS,) + messages.shape[-2:])
    return lax.all_to_all(messages, "sec", split_axis=0, concat_axis=0, tiled=True)


def shift(value, step):
    pairs = [(group, (group + step) % GROUPS) for group in range(GROUPS)]
    return lax.ppermute(value, "mpo", pairs)


def body(wavefunction, block_dims, left_env, right_env, task_left, task_term):
    group = lax.axis_index("mpo").astype(jnp.int32).reshape(1)
    carried = first_carry(block_dims, group, wavefunction, right_env, task_left, task_term)
    mixed, weights = first_mix(exchange(carried))
    own, sent = first_left(exchange(mixed), left_env)
    parts = [shift(sent, step) for step in range(1, GROUPS)]
    carried, first_product = second_carry(group, block_dims, right_env, own, parts)
    mixed = second_mix(exchange(carried), weights)
    parts = second_left(group, exchange(mixed), left_env)
    parts = [parts[0]] + [shift(parts[step], step) for step in range(1, GROUPS)]
    second_product = second_sum(group, block_dims, parts)
    return (first_product, second_product)


def solution(mesh):
    in_specs = (
        P("sec", None, None),
        P("sec"),
        P("sec", "mpo", None, None),
        P("sec", "mpo", None, None),
        P("sec", "mpo"),
        P("sec", "mpo"),
    )
    out_specs = (P("sec", "mpo", None), P("sec", "mpo", None))
    return jax.shard_map(body, mesh=mesh, in_specs=in_specs, out_specs=out_specs, check_vma=False)
```

```python
import jax
import jax.numpy as jnp
from jax import lax
from jax.experimental import pallas as pl
from jax.experimental.pallas import tpu as pltpu
from jax.sharding import PartitionSpec as P

BLOCK = 256
SECTORS = 32
GROUPS = 4
TERMS = 6
HALF_TERMS = 3
TASKS = 32
SLAB = 16
SLABS = BLOCK // SLAB
SHARE = BLOCK // GROUPS
LANES = 128
DATA_ROWS = HALF_TERMS * 2 * SLAB
SIDE_ROWS = 8
MIX = SECTORS * SLAB
EPSILON = 1e-06
LIFT = 512.0

F32 = jnp.float32
BF16 = jnp.bfloat16
VMEM = pl.BlockSpec(memory_space=pltpu.VMEM)
SMEM = pl.BlockSpec(memory_space=pltpu.SMEM)
HBM = pl.BlockSpec(memory_space=pltpu.HBM)
PARAMS = pltpu.CompilerParams(vmem_limit_bytes=48 * 1024 * 1024)


def store_carried(term, carried, out_ref):
    half, place = term // HALF_TERMS, term % HALF_TERMS
    carried = carried.astype(BF16)
    for side in range(2):
        row = (place * 2 + side) * SLAB
        part = carried[:, side * LANES : (side + 1) * LANES].reshape(SLABS, SLAB, LANES)
        out_ref[:, half, row : row + SLAB, :] = part


def fetch_kernel(*refs):
    from_refs, to_refs, sems = refs[:4], refs[4:8], refs[8]
    copies = [
        pltpu.make_async_copy(from_ref, to_ref, sems.at[index])
        for index, (from_ref, to_ref) in enumerate(zip(from_refs, to_refs))
    ]
    for copy in copies:
        copy.start()
    for copy in copies:
        copy.wait()


def fetch(*arrays):
    arrays = [pltpu.with_memory_space_constraint(array, pltpu.HBM) for array in arrays]
    return pl.pallas_call(
        fetch_kernel,
        out_shape=[jax.ShapeDtypeStruct(array.shape, array.dtype) for array in arrays],
        in_specs=[HBM] * len(arrays),
        out_specs=[VMEM] * len(arrays),
        scratch_shapes=[pltpu.SemaphoreType.DMA((len(arrays),))],
        compiler_params=PARAMS,
        name="fetch",
    )(*arrays)


def first_carry_kernel(dims_ref, right_ref, vector_ref, left_ref, term_ref, out_ref, live_ref):
    live = dims_ref[0]
    live_ref[...] = jnp.full((8, LANES), live, jnp.int32)
    vector = live_only(vector_ref[0].astype(F32), 0, live).astype(BF16)
    for term in range(TERMS):
        carried = jnp.dot(vector, right_ref[0, term], preferred_element_type=F32)
        store_carried(term, carried, out_ref)
    line = lax.broadcasted_iota(jnp.int32, (LANES, TASKS), 0)
    for half in range(2):
        place = term_ref[...] - half * HALF_TERMS
        inside = (place >= 0) & (place < HALF_TERMS)
        code = jnp.where(inside, left_ref[...] + place * SECTORS, -1)
        named = jnp.where(line == code, 1.0, 0.0).astype(BF16)
        count = lax.dot_general(
            jnp.ones((SIDE_ROWS, TASKS), BF16),
            named,
            (((1,), (1,)), ((), ())),
            preferred_element_type=F32,
        ).astype(BF16)
        for slab in range(SLABS):
            out_ref[slab, half, DATA_ROWS:, :] = count


def first_carry(dims, fetched):
    return pl.pallas_call(
        first_carry_kernel,
        out_shape=(
            jax.ShapeDtypeStruct((SLABS, 2, DATA_ROWS + SIDE_ROWS, LANES), BF16),
            jax.ShapeDtypeStruct((8, LANES), jnp.int32),
        ),
        in_specs=[SMEM] + [VMEM] * 4,
        out_specs=(VMEM, VMEM),
        compiler_params=PARAMS,
        name="first_carry",
    )(dims, *fetched)


def mix_with(weights_ref, in_ref, out_ref, scale):
    for place in range(HALF_TERMS):
        parts = []
        for side in range(2):
            row = (place * 2 + side) * SLAB
            parts.append(in_ref[:, row : row + SLAB, :].reshape(MIX, LANES))
        mixed = jnp.dot(
            weights_ref[place], jnp.concatenate(parts, axis=1), preferred_element_type=F32
        )
        if scale is not None:
            mixed = jnp.where(scale > 0.0, mixed * scale, 0.0)
        mixed = mixed.astype(BF16).reshape(SECTORS, SLAB, BLOCK)
        out_ref[:, place * SLAB : (place + 1) * SLAB, :] = mixed


def first_mix_kernel(in_ref, out_ref, weights_ref, wide_ref):
    counts = in_ref[:, DATA_ROWS:, :].reshape(SECTORS * SIDE_ROWS, LANES)
    sent_row = lax.broadcasted_iota(jnp.int32, (SECTORS * SIDE_ROWS, MIX), 0)
    mixed_row = lax.broadcasted_iota(jnp.int32, (SECTORS * SIDE_ROWS, MIX), 1)
    spread = sent_row == mixed_row // SLAB * SIDE_ROWS
    spread = jnp.where(spread, 1.0, 0.0).astype(BF16)
    wide_ref[...] = lax.dot_general(
        counts, spread, (((0,), (0,)), ((), ())), preferred_element_type=F32
    )
    same_row = (
        lax.broadcasted_iota(jnp.int32, (SLAB, MIX), 0)
        == lax.broadcasted_iota(jnp.int32, (SLAB, MIX), 1) % SLAB
    )
    same_row = jnp.where(same_row, 1.0, 0.0)
    for place in range(HALF_TERMS):
        for target in range(SECTORS):
            line = place * SECTORS + target
            weights_ref[place, target * SLAB : (target + 1) * SLAB, :] = (
                same_row * wide_ref[line : line + 1, :]
            ).astype(BF16)
    mix_with(weights_ref, in_ref, out_ref, None)


def first_mix(received):
    return pl.pallas_call(
        first_mix_kernel,
        out_shape=(
            jax.ShapeDtypeStruct((SECTORS, HALF_TERMS * SLAB, BLOCK), BF16),
            jax.ShapeDtypeStruct((HALF_TERMS, MIX, MIX), BF16),
        ),
        in_specs=[VMEM],
        out_specs=(VMEM, VMEM),
        scratch_shapes=[pltpu.VMEM((LANES, MIX), F32)],
        compiler_params=PARAMS,
        name="first_mix",
    )(received)


def second_mix_kernel(in_ref, weights_ref, out_ref):
    pieces = in_ref[:, DATA_ROWS : DATA_ROWS + SIDE_ROWS, :].astype(F32)
    mean = jnp.sum(pieces, keepdims=True)[0]
    inverse_rms = lax.rsqrt(mean + EPSILON) * (1.0 / LIFT)
    mix_with(weights_ref, in_ref, out_ref, inverse_rms)


def second_mix(received, weights):
    return pl.pallas_call(
        second_mix_kernel,
        out_shape=jax.ShapeDtypeStruct((SECTORS, HALF_TERMS * SLAB, BLOCK), BF16),
        in_specs=[VMEM, VMEM],
        out_specs=VMEM,
        compiler_params=PARAMS,
        name="second_mix",
    )(received, weights)


def left_product(in_ref, left_ref):
    value = jnp.zeros((BLOCK, BLOCK), F32)
    for term in range(TERMS):
        half, place = term // HALF_TERMS, term % HALF_TERMS
        mixed = in_ref[:, half, place * SLAB : (place + 1) * SLAB, :].reshape(BLOCK, BLOCK)
        value += jnp.dot(left_ref[0, term], mixed, preferred_element_type=F32)
    return value


def first_left_kernel(in_ref, left_ref, own_ref, sent_ref):
    value = left_product(in_ref, left_ref)
    own_ref[...] = value
    sent_ref[...] = value.astype(BF16)


def first_left(received, left_env):
    return pl.pallas_call(
        first_left_kernel,
        out_shape=(
            jax.ShapeDtypeStruct((BLOCK, BLOCK), F32),
            jax.ShapeDtypeStruct((BLOCK, BLOCK), BF16),
        ),
        in_specs=[VMEM, VMEM],
        out_specs=(VMEM, VMEM),
        compiler_params=PARAMS,
        name="first_left",
    )(received.reshape(SLABS, 2, HALF_TERMS * SLAB, BLOCK), left_env)


def second_left_kernel(in_ref, left_ref, *refs):
    *out_refs, total = refs
    group = lax.axis_index("mpo")
    total[...] = left_product(in_ref, left_ref)
    for step in range(GROUPS):
        owner = lax.rem(group + step, GROUPS)
        part = total[pl.ds(pl.multiple_of(owner * SHARE, SHARE), SHARE), :]
        out_refs[step][...] = part.astype(out_refs[step].dtype)


def second_left(received, left_env):
    own = jax.ShapeDtypeStruct((SHARE, BLOCK), F32)
    sent = jax.ShapeDtypeStruct((SHARE, BLOCK), BF16)
    return pl.pallas_call(
        second_left_kernel,
        out_shape=(own,) + (sent,) * (GROUPS - 1),
        in_specs=[VMEM, VMEM],
        out_specs=(VMEM,) * GROUPS,
        scratch_shapes=[pltpu.VMEM((BLOCK, BLOCK), F32)],
        compiler_params=PARAMS,
        name="second_left",
    )(received.reshape(SLABS, 2, HALF_TERMS * SLAB, BLOCK), left_env)


def live_only(value, first_row, live):
    rows = lax.broadcasted_iota(jnp.int32, value.shape, 0) + first_row
    cols = lax.broadcasted_iota(jnp.int32, value.shape, 1)
    return jnp.where((rows < live) & (cols < live), value, 0.0)


def second_carry_kernel(live_ref, right_ref, own_ref, *refs):
    *part_refs, out_ref, first_hbm, total, sem = refs
    value = own_ref[...]
    for part_ref in part_refs:
        value += part_ref[...].astype(F32)
    value = live_only(value, 0, live_ref[:1, :1])
    total[...] = value
    first_row = pl.multiple_of(lax.axis_index("mpo") * SHARE, SHARE)
    copy = pltpu.make_async_copy(total.at[pl.ds(first_row, SHARE), :], first_hbm.at[0], sem)
    copy.start()
    mean = jnp.sum(value * value, keepdims=True) * (1.0 / (SECTORS * BLOCK * BLOCK))
    high = mean.astype(BF16)
    rest = jnp.where(mean < jnp.inf, mean - high.astype(F32), 0.0)
    middle = rest.astype(BF16)
    low = (rest - middle.astype(F32)).astype(BF16)
    lane = lax.broadcasted_iota(jnp.int32, (SIDE_ROWS, LANES), 1)
    row = lax.broadcasted_iota(jnp.int32, (SIDE_ROWS, LANES), 0)
    pieces = jnp.where(lane == 0, high.astype(F32), 0.0)
    pieces = jnp.where(lane == 1, middle.astype(F32), pieces)
    pieces = jnp.where(lane == 2, low.astype(F32), pieces)
    pieces = jnp.where(row == 0, pieces, 0.0).astype(BF16)
    for slab in range(SLABS):
        for half in range(2):
            out_ref[slab, half, DATA_ROWS:, :] = pieces
    lifted = value * LIFT
    upper = lifted.astype(BF16)
    lower = (lifted - upper.astype(F32)).astype(BF16)
    both = jnp.concatenate([upper, lower], axis=0)
    for term in range(TERMS):
        carried = jnp.dot(both, right_ref[0, term], preferred_element_type=F32)
        store_carried(term, carried[:BLOCK] + carried[BLOCK:], out_ref)
    copy.wait()


def second_carry(live, right, own, parts):
    return pl.pallas_call(
        second_carry_kernel,
        out_shape=(
            jax.ShapeDtypeStruct((SLABS, 2, DATA_ROWS + SIDE_ROWS, LANES), BF16),
            jax.ShapeDtypeStruct((1, SHARE, BLOCK), F32),
        ),
        in_specs=[VMEM] * (GROUPS + 2),
        out_specs=(VMEM, HBM),
        scratch_shapes=[pltpu.VMEM((BLOCK, BLOCK), F32), pltpu.SemaphoreType.DMA],
        compiler_params=PARAMS,
        name="second_carry",
    )(live, right, own, *parts)


def second_sum_kernel(live_ref, *refs):
    *part_refs, out_ref = refs
    value = part_refs[0][...]
    for part_ref in part_refs[1:]:
        value += part_ref[...].astype(F32)
    out_ref[0] = live_only(value, lax.axis_index("mpo") * SHARE, live_ref[:1, :1])


def second_sum(live, parts):
    return pl.pallas_call(
        second_sum_kernel,
        out_shape=jax.ShapeDtypeStruct((1, SHARE, BLOCK), F32),
        in_specs=[VMEM] * (GROUPS + 1),
        out_specs=VMEM,
        compiler_params=PARAMS,
        name="second_sum",
    )(live, *parts)


def exchange(messages):
    messages = messages.reshape((SECTORS,) + messages.shape[-2:])
    return lax.all_to_all(messages, "sec", split_axis=0, concat_axis=0, tiled=True)


def shift(value, step):
    pairs = [(group, (group + step) % GROUPS) for group in range(GROUPS)]
    return lax.ppermute(value, "mpo", pairs)


def body(wavefunction, block_dims, left_env, right_env, task_left, task_term):
    fetched = fetch(right_env, wavefunction, task_left, task_term)
    carried, live = first_carry(block_dims, fetched)
    mixed, weights = first_mix(exchange(carried))
    own, sent = first_left(exchange(mixed), left_env)
    parts = [shift(sent, step) for step in (2, 3, 1)]
    carried, first_product = second_carry(live, fetched[0], own, parts)
    mixed = second_mix(exchange(carried), weights)
    parts = second_left(exchange(mixed), left_env)
    parts = [parts[0]] + [shift(parts[step], step) for step in (2, 1, 3)]
    second_product = second_sum(live, parts)
    return (first_product, second_product)


def solution(mesh):
    in_specs = (
        P("sec", None, None),
        P("sec"),
        P("sec", "mpo", None, None),
        P("sec", "mpo", None, None),
        P("sec", "mpo"),
        P("sec", "mpo"),
    )
    out_specs = (P("sec", "mpo", None), P("sec", "mpo", None))
    return jax.shard_map(body, mesh=mesh, in_specs=in_specs, out_specs=out_specs, check_vma=False)
```

```python
import jax
import jax.numpy as jnp
from jax import lax
from jax.experimental import pallas as pl
from jax.experimental.pallas import tpu as pltpu
from jax.sharding import PartitionSpec as P

BLOCK = 256
SECTORS = 32
GROUPS = 4
TERMS = 6
HALF_TERMS = 3
TASKS = 32
SLAB = 16
SLABS = BLOCK // SLAB
SHARE = BLOCK // GROUPS
LANES = 128
DATA_ROWS = HALF_TERMS * 2 * SLAB
SIDE_ROWS = 8
PART = 8
MIX = SECTORS * PART
EPSILON = 1e-06
LIFT = 512.0

F32 = jnp.float32
BF16 = jnp.bfloat16
VMEM = pl.BlockSpec(memory_space=pltpu.VMEM)
SMEM = pl.BlockSpec(memory_space=pltpu.SMEM)
HBM = pl.BlockSpec(memory_space=pltpu.HBM)
PARAMS = pltpu.CompilerParams(vmem_limit_bytes=48 * 1024 * 1024)


def store_carried(term, carried, out_ref):
    half, place = term // HALF_TERMS, term % HALF_TERMS
    carried = carried.astype(BF16)
    for side in range(2):
        row = (place * 2 + side) * SLAB
        part = carried[:, side * LANES : (side + 1) * LANES].reshape(SLABS, SLAB, LANES)
        out_ref[:, half, row : row + SLAB, :] = part


def fetch_kernel(*refs):
    from_refs, to_refs, sems = refs[:4], refs[4:8], refs[8]
    copies = [
        pltpu.make_async_copy(from_ref, to_ref, sems.at[index])
        for index, (from_ref, to_ref) in enumerate(zip(from_refs, to_refs))
    ]
    for copy in copies:
        copy.start()
    for copy in copies:
        copy.wait()


def fetch(*arrays):
    arrays = [pltpu.with_memory_space_constraint(array, pltpu.HBM) for array in arrays]
    return pl.pallas_call(
        fetch_kernel,
        out_shape=[jax.ShapeDtypeStruct(array.shape, array.dtype) for array in arrays],
        in_specs=[HBM] * len(arrays),
        out_specs=[VMEM] * len(arrays),
        scratch_shapes=[pltpu.SemaphoreType.DMA((len(arrays),))],
        compiler_params=PARAMS,
        name="fetch",
    )(*arrays)


def first_carry_kernel(dims_ref, right_ref, vector_ref, left_ref, term_ref, out_ref, live_ref):
    live = dims_ref[0]
    live_ref[...] = jnp.full((8, LANES), live, jnp.int32)
    vector = live_only(vector_ref[0].astype(F32), 0, live).astype(BF16)
    for term in range(TERMS):
        carried = jnp.dot(vector, right_ref[0, term], preferred_element_type=F32)
        store_carried(term, carried, out_ref)
    line = lax.broadcasted_iota(jnp.int32, (LANES, TASKS), 0)
    for half in range(2):
        place = term_ref[...] - half * HALF_TERMS
        inside = (place >= 0) & (place < HALF_TERMS)
        code = jnp.where(inside, left_ref[...] + place * SECTORS, -1)
        named = jnp.where(line == code, 1.0, 0.0).astype(BF16)
        count = lax.dot_general(
            jnp.ones((SIDE_ROWS, TASKS), BF16),
            named,
            (((1,), (1,)), ((), ())),
            preferred_element_type=F32,
        ).astype(BF16)
        for slab in range(SLABS):
            out_ref[slab, half, DATA_ROWS:, :] = count


def first_carry(dims, fetched):
    return pl.pallas_call(
        first_carry_kernel,
        out_shape=(
            jax.ShapeDtypeStruct((SLABS, 2, DATA_ROWS + SIDE_ROWS, LANES), BF16),
            jax.ShapeDtypeStruct((8, LANES), jnp.int32),
        ),
        in_specs=[SMEM] + [VMEM] * 4,
        out_specs=(VMEM, VMEM),
        compiler_params=PARAMS,
        name="first_carry",
    )(dims, *fetched)


def mix_with(weights_ref, in_ref, out_ref, scale):
    for place in range(HALF_TERMS):
        for start in range(0, SLAB, PART):
            sides = []
            for side in range(2):
                row = (place * 2 + side) * SLAB + start
                sides.append(in_ref[:, row : row + PART, :].reshape(MIX, LANES))
            mixed = jnp.dot(
                weights_ref[place], jnp.concatenate(sides, axis=1), preferred_element_type=F32
            )
            if scale is not None:
                mixed = jnp.where(scale > 0.0, mixed * scale, 0.0)
            row = place * SLAB + start
            out_ref[:, row : row + PART, :] = mixed.astype(BF16).reshape(SECTORS, PART, BLOCK)


def first_mix_kernel(in_ref, out_ref, weights_ref, wide_ref):
    counts = in_ref[:, DATA_ROWS:, :].reshape(SECTORS * SIDE_ROWS, LANES)
    sent_row = lax.broadcasted_iota(jnp.int32, (SECTORS * SIDE_ROWS, MIX), 0)
    mixed_row = lax.broadcasted_iota(jnp.int32, (SECTORS * SIDE_ROWS, MIX), 1)
    spread = sent_row == mixed_row // PART * SIDE_ROWS
    spread = jnp.where(spread, 1.0, 0.0).astype(BF16)
    wide_ref[...] = lax.dot_general(
        counts, spread, (((0,), (0,)), ((), ())), preferred_element_type=F32
    )
    same_row = (
        lax.broadcasted_iota(jnp.int32, (PART, MIX), 0)
        == lax.broadcasted_iota(jnp.int32, (PART, MIX), 1) % PART
    )
    same_row = jnp.where(same_row, 1.0, 0.0)
    for place in range(HALF_TERMS):
        for target in range(0, SECTORS, 2):
            line = place * SECTORS + target
            both = [same_row * wide_ref[line + k : line + k + 1, :] for k in range(2)]
            weights_ref[place, target * PART : (target + 2) * PART, :] = jnp.concatenate(
                both, axis=0
            ).astype(BF16)
    mix_with(weights_ref, in_ref, out_ref, None)


def first_mix(received):
    return pl.pallas_call(
        first_mix_kernel,
        out_shape=(
            jax.ShapeDtypeStruct((SECTORS, HALF_TERMS * SLAB, BLOCK), BF16),
            jax.ShapeDtypeStruct((HALF_TERMS, MIX, MIX), BF16),
        ),
        in_specs=[VMEM],
        out_specs=(VMEM, VMEM),
        scratch_shapes=[pltpu.VMEM((LANES, MIX), F32)],
        compiler_params=PARAMS,
        name="first_mix",
    )(received)


def second_mix_kernel(in_ref, weights_ref, out_ref):
    pieces = in_ref[:, DATA_ROWS : DATA_ROWS + SIDE_ROWS, :].astype(F32)
    mean = jnp.sum(pieces, keepdims=True)[0]
    inverse_rms = lax.rsqrt(mean + EPSILON) * (1.0 / LIFT)
    mix_with(weights_ref, in_ref, out_ref, inverse_rms)


def second_mix(received, weights):
    return pl.pallas_call(
        second_mix_kernel,
        out_shape=jax.ShapeDtypeStruct((SECTORS, HALF_TERMS * SLAB, BLOCK), BF16),
        in_specs=[VMEM, VMEM],
        out_specs=VMEM,
        compiler_params=PARAMS,
        name="second_mix",
    )(received, weights)


def left_product(in_ref, left_ref):
    value = jnp.zeros((BLOCK, BLOCK), F32)
    for term in range(TERMS):
        half, place = term // HALF_TERMS, term % HALF_TERMS
        mixed = in_ref[:, half, place * SLAB : (place + 1) * SLAB, :].reshape(BLOCK, BLOCK)
        value += jnp.dot(left_ref[0, term], mixed, preferred_element_type=F32)
    return value


def first_left_kernel(in_ref, left_ref, own_ref, sent_ref):
    value = left_product(in_ref, left_ref)
    own_ref[...] = value
    sent_ref[...] = value.astype(BF16)


def first_left(received, left_env):
    return pl.pallas_call(
        first_left_kernel,
        out_shape=(
            jax.ShapeDtypeStruct((BLOCK, BLOCK), F32),
            jax.ShapeDtypeStruct((BLOCK, BLOCK), BF16),
        ),
        in_specs=[VMEM, VMEM],
        out_specs=(VMEM, VMEM),
        compiler_params=PARAMS,
        name="first_left",
    )(received.reshape(SLABS, 2, HALF_TERMS * SLAB, BLOCK), left_env)


def second_left_kernel(in_ref, left_ref, *refs):
    *out_refs, total = refs
    group = lax.axis_index("mpo")
    total[...] = left_product(in_ref, left_ref)
    for step in range(GROUPS):
        owner = lax.rem(group + step, GROUPS)
        part = total[pl.ds(pl.multiple_of(owner * SHARE, SHARE), SHARE), :]
        out_refs[step][...] = part.astype(out_refs[step].dtype)


def second_left(received, left_env):
    own = jax.ShapeDtypeStruct((SHARE, BLOCK), F32)
    sent = jax.ShapeDtypeStruct((SHARE, BLOCK), BF16)
    return pl.pallas_call(
        second_left_kernel,
        out_shape=(own,) + (sent,) * (GROUPS - 1),
        in_specs=[VMEM, VMEM],
        out_specs=(VMEM,) * GROUPS,
        scratch_shapes=[pltpu.VMEM((BLOCK, BLOCK), F32)],
        compiler_params=PARAMS,
        name="second_left",
    )(received.reshape(SLABS, 2, HALF_TERMS * SLAB, BLOCK), left_env)


def live_only(value, first_row, live):
    rows = lax.broadcasted_iota(jnp.int32, value.shape, 0) + first_row
    cols = lax.broadcasted_iota(jnp.int32, value.shape, 1)
    return jnp.where((rows < live) & (cols < live), value, 0.0)


def second_carry_kernel(live_ref, right_ref, own_ref, *refs):
    *part_refs, out_ref, share_ref, total = refs
    value = own_ref[...]
    for part_ref in part_refs:
        value += part_ref[...].astype(F32)
    value = live_only(value, 0, live_ref[:1, :1])
    total[...] = value
    first_row = pl.multiple_of(lax.axis_index("mpo") * SHARE, SHARE)
    share_ref[...] = total[pl.ds(first_row, SHARE), :]
    mean = jnp.sum(value * value, keepdims=True) * (1.0 / (SECTORS * BLOCK * BLOCK))
    high = mean.astype(BF16)
    rest = jnp.where(mean < jnp.inf, mean - high.astype(F32), 0.0)
    middle = rest.astype(BF16)
    low = (rest - middle.astype(F32)).astype(BF16)
    lane = lax.broadcasted_iota(jnp.int32, (SIDE_ROWS, LANES), 1)
    row = lax.broadcasted_iota(jnp.int32, (SIDE_ROWS, LANES), 0)
    pieces = jnp.where(lane == 0, high.astype(F32), 0.0)
    pieces = jnp.where(lane == 1, middle.astype(F32), pieces)
    pieces = jnp.where(lane == 2, low.astype(F32), pieces)
    pieces = jnp.where(row == 0, pieces, 0.0).astype(BF16)
    for slab in range(SLABS):
        for half in range(2):
            out_ref[slab, half, DATA_ROWS:, :] = pieces
    lifted = value * LIFT
    upper = lifted.astype(BF16)
    lower = (lifted - upper.astype(F32)).astype(BF16)
    both = jnp.concatenate([upper, lower], axis=0)
    for term in range(TERMS):
        carried = jnp.dot(both, right_ref[0, term], preferred_element_type=F32)
        store_carried(term, carried[:BLOCK] + carried[BLOCK:], out_ref)


def second_carry(live, right, own, parts):
    return pl.pallas_call(
        second_carry_kernel,
        out_shape=(
            jax.ShapeDtypeStruct((SLABS, 2, DATA_ROWS + SIDE_ROWS, LANES), BF16),
            jax.ShapeDtypeStruct((SHARE, BLOCK), F32),
        ),
        in_specs=[VMEM] * (GROUPS + 2),
        out_specs=(VMEM, VMEM),
        scratch_shapes=[pltpu.VMEM((BLOCK, BLOCK), F32)],
        compiler_params=PARAMS,
        name="second_carry",
    )(live, right, own, *parts)


def outputs_kernel(live_ref, share_ref, *refs):
    *part_refs, first_hbm, second_hbm, total, sems = refs
    first_copy = pltpu.make_async_copy(share_ref, first_hbm.at[0], sems.at[0])
    first_copy.start()
    value = part_refs[0][...]
    for part_ref in part_refs[1:]:
        value += part_ref[...].astype(F32)
    total[...] = live_only(value, lax.axis_index("mpo") * SHARE, live_ref[:1, :1])
    second_copy = pltpu.make_async_copy(total, second_hbm.at[0], sems.at[1])
    second_copy.start()
    first_copy.wait()
    second_copy.wait()


def outputs(live, share, parts):
    result = jax.ShapeDtypeStruct((1, SHARE, BLOCK), F32)
    return pl.pallas_call(
        outputs_kernel,
        out_shape=(result, result),
        in_specs=[VMEM] * (GROUPS + 2),
        out_specs=(HBM, HBM),
        scratch_shapes=[pltpu.VMEM((SHARE, BLOCK), F32), pltpu.SemaphoreType.DMA((2,))],
        compiler_params=PARAMS,
        name="outputs",
    )(live, share, *parts)


def exchange(messages):
    messages = messages.reshape((SECTORS,) + messages.shape[-2:])
    return lax.all_to_all(messages, "sec", split_axis=0, concat_axis=0, tiled=True)


def shift(value, step):
    pairs = [(group, (group + step) % GROUPS) for group in range(GROUPS)]
    return lax.ppermute(value, "mpo", pairs)


def body(wavefunction, block_dims, left_env, right_env, task_left, task_term):
    fetched = fetch(right_env, wavefunction, task_left, task_term)
    carried, live = first_carry(block_dims, fetched)
    mixed, weights = first_mix(exchange(carried))
    own, sent = first_left(exchange(mixed), left_env)
    parts = [shift(sent, step) for step in (2, 3, 1)]
    carried, share = second_carry(live, fetched[0], own, parts)
    mixed = second_mix(exchange(carried), weights)
    parts = second_left(exchange(mixed), left_env)
    parts = [parts[0]] + [shift(parts[step], step) for step in (2, 1, 3)]
    return outputs(live, share, parts)


def solution(mesh):
    in_specs = (
        P("sec", None, None),
        P("sec"),
        P("sec", "mpo", None, None),
        P("sec", "mpo", None, None),
        P("sec", "mpo"),
        P("sec", "mpo"),
    )
    out_specs = (P("sec", "mpo", None), P("sec", "mpo", None))
    return jax.shard_map(body, mesh=mesh, in_specs=in_specs, out_specs=out_specs, check_vma=False)
```

```python
import jax
import jax.numpy as jnp
from jax import lax
from jax.experimental import pallas as pl
from jax.experimental.pallas import tpu as pltpu
from jax.sharding import PartitionSpec as P

BLOCK = 256
SECTORS = 32
GROUPS = 4
TERMS = 6
HALF_TERMS = 3
TASKS = 32
SLAB = 16
SLABS = BLOCK // SLAB
SHARE = BLOCK // GROUPS
LANES = 128
DATA_ROWS = HALF_TERMS * 2 * SLAB
SIDE_ROWS = 8
PART = 8
MIX = SECTORS * PART
EPSILON = 1e-06
LIFT = 512.0

F32 = jnp.float32
BF16 = jnp.bfloat16
VMEM = pl.BlockSpec(memory_space=pltpu.VMEM)
SMEM = pl.BlockSpec(memory_space=pltpu.SMEM)
HBM = pl.BlockSpec(memory_space=pltpu.HBM)
PARAMS = pltpu.CompilerParams(vmem_limit_bytes=48 * 1024 * 1024)


def store_carried(term, carried, out_ref):
    half, place = term // HALF_TERMS, term % HALF_TERMS
    carried = carried.astype(BF16)
    for side in range(2):
        row = (place * 2 + side) * SLAB
        part = carried[:, side * LANES : (side + 1) * LANES].reshape(SLABS, SLAB, LANES)
        out_ref[:, half, row : row + SLAB, :] = part


def fetch_kernel(*refs):
    from_refs, to_refs, sems = refs[:4], refs[4:8], refs[8]
    copies = [
        pltpu.make_async_copy(from_ref, to_ref, sems.at[index])
        for index, (from_ref, to_ref) in enumerate(zip(from_refs, to_refs))
    ]
    for copy in copies:
        copy.start()
    for copy in copies:
        copy.wait()


def fetch(*arrays):
    arrays = [pltpu.with_memory_space_constraint(array, pltpu.HBM) for array in arrays]
    return pl.pallas_call(
        fetch_kernel,
        out_shape=[jax.ShapeDtypeStruct(array.shape, array.dtype) for array in arrays],
        in_specs=[HBM] * len(arrays),
        out_specs=[VMEM] * len(arrays),
        scratch_shapes=[pltpu.SemaphoreType.DMA((len(arrays),))],
        compiler_params=PARAMS,
        name="fetch",
    )(*arrays)


def first_carry_kernel(dims_ref, right_ref, vector_ref, left_ref, term_ref, out_ref, live_ref):
    live = dims_ref[0]
    live_ref[...] = jnp.full((8, LANES), live, jnp.int32)
    vector = live_only(vector_ref[0].astype(F32), 0, live).astype(BF16)
    for term in range(TERMS):
        carried = jnp.dot(vector, right_ref[0, term], preferred_element_type=F32)
        store_carried(term, carried, out_ref)
    line = lax.broadcasted_iota(jnp.int32, (LANES, TASKS), 0)
    for half in range(2):
        place = term_ref[...] - half * HALF_TERMS
        inside = (place >= 0) & (place < HALF_TERMS)
        code = jnp.where(inside, left_ref[...] + place * SECTORS, -1)
        named = jnp.where(line == code, 1.0, 0.0).astype(BF16)
        count = lax.dot_general(
            jnp.ones((SIDE_ROWS, TASKS), BF16),
            named,
            (((1,), (1,)), ((), ())),
            preferred_element_type=F32,
        ).astype(BF16)
        for slab in range(SLABS):
            out_ref[slab, half, DATA_ROWS:, :] = count


def first_carry(dims, fetched):
    return pl.pallas_call(
        first_carry_kernel,
        out_shape=(
            jax.ShapeDtypeStruct((SLABS, 2, DATA_ROWS + SIDE_ROWS, LANES), BF16),
            jax.ShapeDtypeStruct((8, LANES), jnp.int32),
        ),
        in_specs=[SMEM] + [VMEM] * 4,
        out_specs=(VMEM, VMEM),
        compiler_params=PARAMS,
        name="first_carry",
    )(dims, *fetched)


def mix_with(weights_ref, in_ref, out_ref, scale):
    for place in range(HALF_TERMS):
        for start in range(0, SLAB, PART):
            sides = []
            for side in range(2):
                row = (place * 2 + side) * SLAB + start
                sides.append(in_ref[:, row : row + PART, :].reshape(MIX, LANES))
            mixed = jnp.dot(
                weights_ref[place], jnp.concatenate(sides, axis=1), preferred_element_type=F32
            )
            if scale is not None:
                mixed = jnp.where(scale > 0.0, mixed * scale, 0.0)
            row = place * SLAB + start
            out_ref[:, row : row + PART, :] = mixed.astype(BF16).reshape(SECTORS, PART, BLOCK)


def first_mix_kernel(in_ref, out_ref, weights_ref, wide_ref):
    counts = in_ref[:, DATA_ROWS:, :].reshape(SECTORS * SIDE_ROWS, LANES)
    sent_row = lax.broadcasted_iota(jnp.int32, (SECTORS * SIDE_ROWS, MIX), 0)
    mixed_row = lax.broadcasted_iota(jnp.int32, (SECTORS * SIDE_ROWS, MIX), 1)
    spread = sent_row == mixed_row // PART * SIDE_ROWS
    spread = jnp.where(spread, 1.0, 0.0).astype(BF16)
    wide_ref[...] = lax.dot_general(
        counts, spread, (((0,), (0,)), ((), ())), preferred_element_type=F32
    )
    same_row = (
        lax.broadcasted_iota(jnp.int32, (PART, MIX), 0)
        == lax.broadcasted_iota(jnp.int32, (PART, MIX), 1) % PART
    )
    same_row = jnp.where(same_row, 1.0, 0.0)
    for place in range(HALF_TERMS):
        for target in range(0, SECTORS, 2):
            line = place * SECTORS + target
            both = [same_row * wide_ref[line + k : line + k + 1, :] for k in range(2)]
            weights_ref[place, target * PART : (target + 2) * PART, :] = jnp.concatenate(
                both, axis=0
            ).astype(BF16)
    mix_with(weights_ref, in_ref, out_ref, None)


def first_mix(received):
    return pl.pallas_call(
        first_mix_kernel,
        out_shape=(
            jax.ShapeDtypeStruct((SECTORS, HALF_TERMS * SLAB, BLOCK), BF16),
            jax.ShapeDtypeStruct((HALF_TERMS, MIX, MIX), BF16),
        ),
        in_specs=[VMEM],
        out_specs=(VMEM, VMEM),
        scratch_shapes=[pltpu.VMEM((LANES, MIX), F32)],
        compiler_params=PARAMS,
        name="first_mix",
    )(received)


def second_mix_kernel(in_ref, weights_ref, out_ref):
    pieces = in_ref[:, DATA_ROWS : DATA_ROWS + SIDE_ROWS, :].astype(F32)
    mean = jnp.sum(pieces, keepdims=True)[0]
    inverse_rms = lax.rsqrt(mean + EPSILON) * (1.0 / LIFT)
    mix_with(weights_ref, in_ref, out_ref, inverse_rms)


def second_mix(received, weights):
    return pl.pallas_call(
        second_mix_kernel,
        out_shape=jax.ShapeDtypeStruct((SECTORS, HALF_TERMS * SLAB, BLOCK), BF16),
        in_specs=[VMEM, VMEM],
        out_specs=VMEM,
        compiler_params=PARAMS,
        name="second_mix",
    )(received, weights)


def left_product(in_ref, left_ref):
    value = jnp.zeros((BLOCK, BLOCK), F32)
    for term in range(TERMS):
        half, place = term // HALF_TERMS, term % HALF_TERMS
        mixed = in_ref[:, half, place * SLAB : (place + 1) * SLAB, :].reshape(BLOCK, BLOCK)
        value += jnp.dot(left_ref[0, term], mixed, preferred_element_type=F32)
    return value


def first_left_kernel(in_ref, left_ref, own_ref, sent_ref):
    value = left_product(in_ref, left_ref)
    own_ref[...] = value
    sent_ref[...] = value.astype(BF16)


def first_left(received, left_env):
    return pl.pallas_call(
        first_left_kernel,
        out_shape=(
            jax.ShapeDtypeStruct((BLOCK, BLOCK), F32),
            jax.ShapeDtypeStruct((BLOCK, BLOCK), BF16),
        ),
        in_specs=[VMEM, VMEM],
        out_specs=(VMEM, VMEM),
        compiler_params=PARAMS,
        name="first_left",
    )(received.reshape(SLABS, 2, HALF_TERMS * SLAB, BLOCK), left_env)


def second_left_kernel(in_ref, left_ref, *refs):
    *out_refs, total = refs
    group = lax.axis_index("mpo")
    total[...] = left_product(in_ref, left_ref)
    for step in range(GROUPS):
        owner = lax.rem(group + step, GROUPS)
        part = total[pl.ds(pl.multiple_of(owner * SHARE, SHARE), SHARE), :]
        out_refs[step][...] = part.astype(out_refs[step].dtype)


def second_left(received, left_env):
    own = jax.ShapeDtypeStruct((SHARE, BLOCK), F32)
    sent = jax.ShapeDtypeStruct((SHARE, BLOCK), BF16)
    return pl.pallas_call(
        second_left_kernel,
        out_shape=(own,) + (sent,) * (GROUPS - 1),
        in_specs=[VMEM, VMEM],
        out_specs=(VMEM,) * GROUPS,
        scratch_shapes=[pltpu.VMEM((BLOCK, BLOCK), F32)],
        compiler_params=PARAMS,
        name="second_left",
    )(received.reshape(SLABS, 2, HALF_TERMS * SLAB, BLOCK), left_env)


def live_only(value, first_row, live):
    rows = lax.broadcasted_iota(jnp.int32, value.shape, 0) + first_row
    cols = lax.broadcasted_iota(jnp.int32, value.shape, 1)
    return jnp.where((rows < live) & (cols < live), value, 0.0)


def second_carry_kernel(live_ref, right_ref, own_ref, *refs):
    *part_refs, out_ref, share_ref, total = refs
    value = own_ref[...]
    for part_ref in part_refs:
        value += part_ref[...].astype(F32)
    value = live_only(value, 0, live_ref[:1, :1])
    total[...] = value
    first_row = pl.multiple_of(lax.axis_index("mpo") * SHARE, SHARE)
    share_ref[...] = total[pl.ds(first_row, SHARE), :]
    lifted = value * LIFT
    upper = lifted.astype(BF16)
    lower = (lifted - upper.astype(F32)).astype(BF16)
    both = jnp.concatenate([upper, lower], axis=0)
    for term in range(TERMS):
        carried = jnp.dot(both, right_ref[0, term], preferred_element_type=F32)
        store_carried(term, carried[:BLOCK] + carried[BLOCK:], out_ref)
    mean = jnp.sum(value * value, keepdims=True) * (1.0 / (SECTORS * BLOCK * BLOCK))
    high = mean.astype(BF16)
    rest = jnp.where(mean < jnp.inf, mean - high.astype(F32), 0.0)
    middle = rest.astype(BF16)
    low = (rest - middle.astype(F32)).astype(BF16)
    lane = lax.broadcasted_iota(jnp.int32, (SIDE_ROWS, LANES), 1)
    row = lax.broadcasted_iota(jnp.int32, (SIDE_ROWS, LANES), 0)
    pieces = jnp.where(lane == 0, high.astype(F32), 0.0)
    pieces = jnp.where(lane == 1, middle.astype(F32), pieces)
    pieces = jnp.where(lane == 2, low.astype(F32), pieces)
    pieces = jnp.where(row == 0, pieces, 0.0).astype(BF16)
    for slab in range(SLABS):
        for half in range(2):
            out_ref[slab, half, DATA_ROWS:, :] = pieces


def second_carry(live, right, own, parts):
    return pl.pallas_call(
        second_carry_kernel,
        out_shape=(
            jax.ShapeDtypeStruct((SLABS, 2, DATA_ROWS + SIDE_ROWS, LANES), BF16),
            jax.ShapeDtypeStruct((SHARE, BLOCK), F32),
        ),
        in_specs=[VMEM] * (GROUPS + 2),
        out_specs=(VMEM, VMEM),
        scratch_shapes=[pltpu.VMEM((BLOCK, BLOCK), F32)],
        compiler_params=PARAMS,
        name="second_carry",
    )(live, right, own, *parts)


def outputs_kernel(live_ref, share_ref, *refs):
    *part_refs, first_hbm, second_hbm, total, sems = refs
    first_copy = pltpu.make_async_copy(share_ref, first_hbm.at[0], sems.at[0])
    first_copy.start()
    value = part_refs[0][...]
    for part_ref in part_refs[1:]:
        value += part_ref[...].astype(F32)
    total[...] = live_only(value, lax.axis_index("mpo") * SHARE, live_ref[:1, :1])
    second_copy = pltpu.make_async_copy(total, second_hbm.at[0], sems.at[1])
    second_copy.start()
    first_copy.wait()
    second_copy.wait()


def outputs(live, share, parts):
    result = jax.ShapeDtypeStruct((1, SHARE, BLOCK), F32)
    return pl.pallas_call(
        outputs_kernel,
        out_shape=(result, result),
        in_specs=[VMEM] * (GROUPS + 2),
        out_specs=(HBM, HBM),
        scratch_shapes=[pltpu.VMEM((SHARE, BLOCK), F32), pltpu.SemaphoreType.DMA((2,))],
        compiler_params=PARAMS,
        name="outputs",
    )(live, share, *parts)


def exchange(messages):
    messages = messages.reshape((SECTORS,) + messages.shape[-2:])
    return lax.all_to_all(messages, "sec", split_axis=0, concat_axis=0, tiled=True)


def shift(value, step):
    pairs = [(group, (group + step) % GROUPS) for group in range(GROUPS)]
    return lax.ppermute(value, "mpo", pairs)


def shift_both_ways(value, step):
    pairs = []
    for sector in range(SECTORS):
        ahead = step if sector % 2 == 0 else GROUPS - step
        for group in range(GROUPS):
            target = (group + ahead) % GROUPS
            pairs.append((sector * GROUPS + group, sector * GROUPS + target))
    return lax.ppermute(value, ("sec", "mpo"), pairs)


def body(wavefunction, block_dims, left_env, right_env, task_left, task_term):
    fetched = fetch(right_env, wavefunction, task_left, task_term)
    carried, live = first_carry(block_dims, fetched)
    mixed, weights = first_mix(exchange(carried))
    own, sent = first_left(exchange(mixed), left_env)
    parts = [shift_both_ways(sent, step) for step in (2, 3, 1)]
    carried, share = second_carry(live, fetched[0], own, parts)
    mixed = second_mix(exchange(carried), weights)
    parts = second_left(exchange(mixed), left_env)
    parts = [parts[0]] + [shift(parts[step], step) for step in (2, 1, 3)]
    return outputs(live, share, parts)


def solution(mesh):
    in_specs = (
        P("sec", None, None),
        P("sec"),
        P("sec", "mpo", None, None),
        P("sec", "mpo", None, None),
        P("sec", "mpo"),
        P("sec", "mpo"),
    )
    out_specs = (P("sec", "mpo", None), P("sec", "mpo", None))
    return jax.shard_map(body, mesh=mesh, in_specs=in_specs, out_specs=out_specs, check_vma=False)
```
